32 devices in a mesh: dp: 4 (over y, core), fsdp: 8 (over z, x).
Axes of the slice: x: 2, y: 2, z: 4, core: 2. Of those that a mesh axis runs over, the one named last changes fastest.
Arguments:
- tokens: bfloat16 [32768, 768], P(('dp', 'fsdp')), may hold values from -6 to 6
- doc_start: int32 [256], P(('dp', 'fsdp')), may hold values from 0 to 7, as said below
- attn_gain: bfloat16 [768], P(('dp', 'fsdp')), may hold values from 0.5 to 1.5
- attn_bias: bfloat16 [768], P(('dp', 'fsdp')), may hold values from -1.5 to 1.5
- w_query: bfloat16 [768, 768], P(('dp', 'fsdp')), may hold values from -0.21875 to 0.21875
- w_key: bfloat16 [768, 768], P(('dp', 'fsdp')), may hold values from -0.21875 to 0.21875
- w_value: bfloat16 [768, 768], P(('dp', 'fsdp')), may hold values from -0.21875 to 0.21875
- shift_taps: bfloat16 [768, 64], P(('dp', 'fsdp')), may hold values from -0.75 to 0.75
- log_step: bfloat16 [768], P(('dp', 'fsdp')), may hold values from -6.875 to -2.296875
- state_out: bfloat16 [768, 64], P(('dp', 'fsdp')), may hold values from -5 to 5
- log_rate: bfloat16 [768, 64], P(('dp', 'fsdp')), may hold values from -0.69921875 to 4.1875
- w_output: bfloat16 [768, 768], P(('dp', 'fsdp')), may hold values from -0.21875 to 0.21875
- mlp_gain: bfloat16 [768], P(('dp', 'fsdp')), may hold values from 0.5 to 1.5
- mlp_bias: bfloat16 [768], P(('dp', 'fsdp')), may hold values from -1.5 to 1.5
- w_up: bfloat16 [768, 3072], P(('dp', 'fsdp')), may hold values from -0.21875 to 0.21875
- w_down: bfloat16 [3072, 768], P(('dp', 'fsdp')), may hold values from -0.109375 to 0.109375
- cotangent: bfloat16 [32768, 768], P(('dp', 'fsdp')), may hold values from -6 to 6
Outputs:
- layer_out: bfloat16 [32768, 768], P(('dp', 'fsdp'))
- tokens_grad: float32 [32768, 768], P(('dp', 'fsdp'))
- attn_gain_grad: float32 [768], P(('dp', 'fsdp'))
- attn_bias_grad: float32 [768], P(('dp', 'fsdp'))
- query_grad: float32 [768, 768], P(('dp', 'fsdp'))
- key_grad: float32 [768, 768], P(('dp', 'fsdp'))
- value_grad: float32 [768, 768], P(('dp', 'fsdp'))
- taps_grad: float32 [768, 64], P(('dp', 'fsdp'))
- step_grad: float32 [768], P(('dp', 'fsdp'))
- state_grad: float32 [768, 64], P(('dp', 'fsdp'))
- rate_grad: float32 [768, 64], P(('dp', 'fsdp'))
- output_grad: float32 [768, 768], P(('dp', 'fsdp'))
- mlp_gain_grad: float32 [768], P(('dp', 'fsdp'))
- mlp_bias_grad: float32 [768], P(('dp', 'fsdp'))
- up_grad: float32 [768, 3072], P(('dp', 'fsdp'))
- down_grad: float32 [3072, 768], P(('dp', 'fsdp'))
The draws below stay inside these ranges and needn't reach their ends.
Inputs may be any that keep to these rules, and one draw needn't show every extreme that they name: `doc_start`: each device's 8 consecutive entries split its blocks into whole sequences of whole blocks: entry i is the first block of the sequence holding block i, so entries never fall within a sequence and equal i at a sequence's start. The first device holds one sequence of 8 blocks and the second 8 sequences of one block.
All inputs are finite; a program needn't handle non-finite values.
Results may differ from the reference program's by a relative error of at most 0.011.
Values may be sent and summed in bfloat16 or wider, within the bound.
A program may use at most 256 MiB of HBM per device.

```python
import jax
import jax.numpy as jnp
from jax import lax

D = 768
FF = 3072
STATE = 64
SHIFT = 64
BLK = 128
NB = 8
BLOCKS = 256
TOKENS = 32768


def draw_doc_start(key, part):
    key = jax.random.fold_in(key, 7)
    device_total = BLOCKS // NB
    kind_key, bound_key = jax.random.split(key)
    device_kind = jax.random.randint(kind_key, (device_total,), 0, 4)
    device_index = jnp.arange(device_total)
    device_kind = jnp.where(device_index == 0, 0, jnp.where(device_index == 1, 1, device_kind))
    boundary_draw = jax.random.randint(bound_key, (device_total, NB), 0, 2)
    bounds = jnp.where(device_kind[:, None] == 0, 0, jnp.where(device_kind[:, None] == 1, 1, boundary_draw))
    places = jnp.arange(NB)[None, :]
    bounds = jnp.where(places == 0, 1, bounds)
    start_marks = jnp.where(bounds == 1, places, 0)
    return lax.cummax(start_marks, axis=1).reshape(-1).astype(jnp.int32)


def shard_levels(key, dims, pieces, low, high):
    level = 1.0
    for axis_at, blocks in pieces:
        heights = jax.random.uniform(jax.random.fold_in(jax.random.fold_in(key, 6), axis_at), (blocks,), jnp.float32, low / len(pieces), high / len(pieces))
        level = level * jnp.repeat(jnp.exp(heights), dims[axis_at] // blocks).reshape((-1,) + (1,) * (len(dims) - 1 - axis_at))
    return level


def gaussian(stream_key, shape, spread, reach, pieces=(), kind=jnp.bfloat16):
    values = spread * jax.random.normal(stream_key, shape, jnp.float32)
    if pieces:
        values = values * shard_levels(stream_key, shape, pieces, -0.22, 0.18)
    return jnp.clip(values, -reach, reach).astype(kind)


def setup_inputs(seed: int = 0) -> dict:
    key_list = jax.random.split(jax.random.key(seed), 18)
    tokens = gaussian(key_list[0], (TOKENS, D), 1.0, 6.0, ((0, 32),))
    doc_start = draw_doc_start(jax.random.fold_in(key_list[17], 71), 0)
    attn_gain = jnp.clip(1.0 + 0.1 * jax.random.normal(key_list[2], (D,), jnp.float32), 0.5, 1.5).astype(jnp.bfloat16)
    attn_bias = gaussian(key_list[3], (D,), 0.3, 1.5, ((0, 32),))
    w_query = gaussian(key_list[4], (D, D), D ** -0.5, 0.21875, ((0, 32),))
    w_key = gaussian(key_list[5], (D, D), D ** -0.5, 0.21875, ((0, 32),))
    w_value = gaussian(key_list[6], (D, D), D ** -0.5, 0.21875, ((0, 32),))
    shift_taps = gaussian(key_list[7], (D, SHIFT), SHIFT ** -0.5, 0.75, ((0, 32),))
    log_step = jnp.clip(-6.875 + 4.578125 * jax.random.uniform(key_list[8], (D,), jnp.float32) ** shard_levels(key_list[8], (D,), ((0, 32),), -0.2, 0.2), -6.875, -2.296875).astype(jnp.bfloat16)
    state_out = gaussian(key_list[9], (D, STATE), 1.0, 5.0, ((0, 32),))
    log_rate = jnp.clip(-0.69921875 + 4.8867188 * jax.random.uniform(key_list[10], (D, STATE), jnp.float32) ** shard_levels(key_list[10], (D, STATE), ((0, 32),), -0.2, 0.2), -0.69921875, 4.1875).astype(jnp.bfloat16)
    w_output = gaussian(key_list[11], (D, D), D ** -0.5, 0.21875, ((0, 32),))
    mlp_gain = jnp.clip(1.0 + 0.1 * jax.random.normal(key_list[12], (D,), jnp.float32), 0.5, 1.5).astype(jnp.bfloat16)
    mlp_bias = gaussian(key_list[13], (D,), 0.3, 1.5, ((0, 32),))
    w_up = gaussian(key_list[14], (D, FF), D ** -0.5, 0.21875, ((0, 32),))
    w_down = gaussian(key_list[15], (FF, D), FF ** -0.5, 0.109375, ((0, 32),))
    cotangent = gaussian(key_list[16], (TOKENS, D), 1.0, 6.0, ((0, 32),))
    return {"tokens": tokens, "doc_start": doc_start, "attn_gain": attn_gain, "attn_bias": attn_bias, "w_query": w_query, "w_key": w_key, "w_value": w_value, "shift_taps": shift_taps, "log_step": log_step, "state_out": state_out, "log_rate": log_rate, "w_output": w_output, "mlp_gain": mlp_gain, "mlp_bias": mlp_bias, "w_up": w_up, "w_down": w_down, "cotangent": cotangent}


@jax.custom_vjp
def low(v):
    return lax.optimization_barrier(v.astype(jnp.bfloat16)).astype(jnp.float32)

@jax.custom_vjp
def low_back(v):
    return v

def low_keep(v):
    return (low(v), None)

def low_pass(kept, grad):
    return (grad,)

def back_keep(v):
    return (v, None)

def back_low(kept, grad):
    return (low(grad),)
low.defvjp(low_keep, low_pass)
low_back.defvjp(back_keep, back_low)

def make_kernel(log_step, state_out, log_rate, blocks, length):
    step_size = jnp.exp(log_step)[:, None]
    decay_rate = step_size * jnp.exp(log_rate)
    weight = state_out * step_size

    def one_block(block_first):
        places = block_first + jnp.arange(length).astype(log_step.dtype)
        decays = jnp.exp(-decay_rate[None, :, :] * places[:, None, None])
        return lax.optimization_barrier(jnp.sum(decays * weight[None, :, :], axis=2))
    block_starts = (jnp.arange(blocks) * length).astype(log_step.dtype)
    return lax.map(jax.checkpoint(one_block), block_starts).reshape(blocks * length, -1)

def conv_blocks(signal, kernel, starts):
    feature_width = signal.shape[1]
    blocks = signal.reshape(NB, BLK, feature_width)
    spectrum = jnp.fft.rfft(blocks, n=2 * BLK, axis=1)
    padded = jnp.concatenate([jnp.zeros((BLK, feature_width), kernel.dtype), kernel], axis=0)
    segments = jnp.concatenate([padded[BLK:].reshape(NB, BLK, feature_width), padded[:NB * BLK].reshape(NB, BLK, feature_width)], axis=1)
    kernel_spec = jnp.fft.rfft(segments, axis=1)
    places = jnp.arange(NB)
    offsets = places[:, None] - places[None, :]
    usable = (offsets >= 0) & (places[None, :] >= starts[:, None])
    chosen = kernel_spec[jnp.clip(offsets, 0, NB - 1)]
    chosen = jnp.where(usable[:, :, None, None], chosen, jnp.zeros_like(chosen))
    combined = jnp.einsum('ijfc,jfc->ifc', chosen, spectrum)
    return jnp.fft.irfft(combined, n=2 * BLK, axis=1)[:, :BLK].reshape(NB * BLK, feature_width)

def layer_norm(values, norm_gain, norm_bias):
    row_mean = lax.optimization_barrier(jnp.mean(values, axis=-1, keepdims=True))
    centred = values - row_mean
    row_var = lax.optimization_barrier(jnp.mean(centred * centred, axis=-1, keepdims=True))
    return centred * lax.rsqrt(row_var + 1e-05) * norm_gain + norm_bias

def product_of(left, right):
    return jnp.dot(left, right, precision=lax.Precision.HIGHEST)

def forward(params, inputs, doc_start):
    attn_gain, attn_bias, w_query, w_key, w_value, shift_taps, log_step, state_out, log_rate, w_output, mlp_gain, mlp_bias, w_up, w_down = params
    positions = NB * BLK
    kernel_long = make_kernel(log_step, state_out, log_rate, NB, BLK)
    kernel_shift = jnp.pad(shift_taps.T, ((0, positions - SHIFT), (0, 0)))
    device_rows = inputs.reshape(-1, positions, D)
    device_starts = doc_start.reshape(-1, NB)

    def one_device(device_pair):
        row_block, starts = device_pair
        normed_one = low(layer_norm(row_block, attn_gain, attn_bias))
        query = low_back(product_of(normed_one, w_query))
        keyed = low_back(product_of(normed_one, w_key))
        valued = low_back(product_of(normed_one, w_value))
        shifted = conv_blocks(keyed, kernel_shift, starts)
        mixed = conv_blocks(shifted * valued, kernel_long, starts)
        gated = low(query * mixed)
        branch = low_back(product_of(gated, w_output))
        middle = row_block + branch
        normed_two = low(layer_norm(middle, mlp_gain, mlp_bias))
        hidden = low_back(product_of(normed_two, w_up))
        active = low(jax.nn.gelu(hidden, approximate=False))
        result = low_back(product_of(active, w_down))
        return middle + result
    outputs = lax.map(jax.checkpoint(one_device), (device_rows, device_starts))
    return outputs.reshape(-1, D)

def reference(tokens, doc_start, attn_gain, attn_bias, w_query, w_key, w_value, shift_taps, log_step, state_out, log_rate, w_output, mlp_gain, mlp_bias, w_up, w_down, cotangent):
    params = tuple((item.astype(jnp.float32) for item in (attn_gain, attn_bias, w_query, w_key, w_value, shift_taps, log_step, state_out, log_rate, w_output, mlp_gain, mlp_bias, w_up, w_down)))
    inputs = tokens.astype(jnp.float32)

    def apply_layer(param_set, input_rows):
        return forward(param_set, input_rows, doc_start)
    outputs, pullback = jax.vjp(apply_layer, params, inputs)
    param_grads, input_grad = pullback(cotangent.astype(jnp.float32))
    return (outputs.astype(jnp.bfloat16), input_grad, param_grads[0], param_grads[1], param_grads[2], param_grads[3], param_grads[4], param_grads[5], param_grads[6], param_grads[7], param_grads[8], param_grads[9], param_grads[10], param_grads[11], param_grads[12], param_grads[13])
```

```python
from functools import partial
import math

import jax
import jax.numpy as jnp
from jax import lax
from jax.experimental import pallas as pl
from jax.experimental.pallas import tpu as pltpu
from jax.sharding import PartitionSpec as P

VMEM_LIMIT = 56 * 1024 * 1024

ORDERS = ("aby", "bya", "yab", "aby", "bya", "yab", "aby", "bya")


MESH = pl.DeviceIdType.MESH


def mesh_dims(dp_size, fsdp_size):
    inner = 8 if fsdp_size == 32 else 2
    return {"y": dp_size // 2, "c": 2, "a": fsdp_size // inner, "b": inner}


def kernels_fit(sizes, rows):
    return rows % 8 == 0 and all(sizes[d] in (1, 2, 4) for d in "yab")


class Place:
    def __init__(self, sizes):
        self.sizes = sizes
        dp, fsdp = lax.axis_index("dp"), lax.axis_index("fsdp")
        self.at = {
            "y": dp // 2,
            "c": dp % 2,
            "a": fsdp // sizes["b"],
            "b": fsdp % sizes["b"],
        }

    def device(self, dim, index):
        at = dict(self.at)
        at[dim] = index
        return (at["y"] * 2 + at["c"], at["a"] * self.sizes["b"] + at["b"])

    def shift(self, dim, step):
        n = self.sizes[dim]
        return (self.at[dim] + (step + n)) % n

    def greet(self):
        barrier = pltpu.get_barrier_semaphore()
        count = 0
        for dim in "ycab":
            n = self.sizes[dim]
            steps = () if n == 1 else (1,) if n == 2 else (1, -1)
            for step in steps:
                pl.semaphore_signal(
                    barrier,
                    inc=1,
                    device_id=self.device(dim, self.shift(dim, step)),
                    device_id_type=MESH,
                )
                count += 1
        pl.semaphore_wait(barrier, count)

    def view(self, buf, known, columns=None):
        index = []
        for dim in "ycab":
            if dim in known:
                index.append(pl.ds(known[dim], 1))
            else:
                index.append(pl.ds(0, self.sizes[dim]))
        if columns is not None:
            index += [slice(None), pl.ds(columns[0], columns[1])]
        return buf.at[tuple(index)]


class Links:
    def __init__(self, send_sem, recv_sem):
        self.send_sem, self.recv_sem, self.used = send_sem, recv_sem, 0

    def copy(self, src, dst, device):
        copy = pltpu.make_async_remote_copy(
            src_ref=src,
            dst_ref=dst,
            send_sem=self.send_sem.at[self.used],
            recv_sem=self.recv_sem.at[self.used],
            device_id=device,
            device_id_type=MESH,
        )
        self.used += 1
        copy.start()
        return copy


def gather_steps(place, links, own, buf, order, local_sem):
    sizes, at = place.sizes, place.at
    columns = buf.shape[-1]
    half = columns // 2
    mine = {d: at[d] for d in "ycab"}
    local = pltpu.make_async_copy(own, buf.at[at["y"], at["c"], at["a"], at["b"]], local_sem)
    local.start()
    own_done = False
    passed = []
    other = place.device("c", 1 - at["c"])

    def give(known):
        passed.append(links.copy(place.view(buf, known), place.view(buf, known), other))

    local.wait()
    give(mine)
    known = dict(mine)
    for dim in order:
        n = sizes[dim]
        if n == 1:
            known.pop(dim)
            continue
        if n == 2:
            copy = links.copy(
                place.view(buf, known), place.view(buf, known), place.device(dim, 1 - at[dim])
            )
            yield
            copy.wait()
            arrived = dict(known)
            arrived[dim] = 1 - at[dim]
            give(arrived)
            known.pop(dim)
            continue
        right, left = place.shift(dim, 1), place.shift(dim, -1)
        to_right, to_left = place.device(dim, right), place.device(dim, left)
        first = links.copy(place.view(buf, known), place.view(buf, known), to_right)
        second = links.copy(place.view(buf, known), place.view(buf, known), to_left)
        yield
        first.wait()
        second.wait()
        from_left, from_right, far = dict(known), dict(known), dict(known)
        from_left[dim], from_right[dim], far[dim] = left, right, place.shift(dim, 2)
        third = links.copy(
            place.view(buf, from_left, (0, half)), place.view(buf, from_left, (0, half)), to_right
        )
        fourth = links.copy(
            place.view(buf, from_right, (half, half)),
            place.view(buf, from_right, (half, half)),
            to_left,
        )
        give(from_left)
        give(from_right)
        yield
        third.wait()
        fourth.wait()
        give(far)
        known.pop(dim)
    yield
    for copy in passed:
        copy.wait()


def run_all(steps):
    active = list(steps)
    while active:
        left = []
        for step in active:
            if next(step, StopIteration) is not StopIteration:
                left.append(step)
        active = left


GATHER_COPIES = 12


def gather_kernel(sizes, orders, *refs):
    count = len(orders)
    owns, bufs = refs[:count], refs[count : 2 * count]
    send_sem, recv_sem, local_sem = refs[2 * count :]
    place = Place(sizes)
    place.greet()
    links = Links(send_sem, recv_sem)
    run_all(
        gather_steps(place, links, owns[i], bufs[i], orders[i], local_sem.at[i])
        for i in range(count)
    )


def gather_all(sizes, arrays, orders, collective_id):
    count = len(arrays)
    lead = (sizes["y"], 2, sizes["a"], sizes["b"])
    total = GATHER_COPIES * count
    moved = sum(a.size for a in arrays) * 2 * math.prod(lead)
    bufs = pl.pallas_call(
        partial(gather_kernel, sizes, orders),
        out_shape=[jax.ShapeDtypeStruct(lead + a.shape, a.dtype) for a in arrays],
        in_specs=[pl.BlockSpec(memory_space=pl.ANY)] * count,
        out_specs=[pl.BlockSpec(memory_space=pl.ANY)] * count,
        scratch_shapes=[
            pltpu.SemaphoreType.DMA((total,)),
            pltpu.SemaphoreType.DMA((total,)),
            pltpu.SemaphoreType.DMA((count,)),
        ],
        compiler_params=pltpu.CompilerParams(collective_id=collective_id, has_side_effects=True),
        cost_estimate=pl.CostEstimate(flops=0, bytes_accessed=moved, transcendentals=0),
    )(*arrays)
    return [b.reshape((-1,) + b.shape[5:]) for b in bufs]


def add_into(total, more, out=None):
    lead = total.shape[:-2]
    for flat in range(math.prod(lead)):
        index = []
        rest = flat
        for n in reversed(lead):
            index.append(rest % n)
            rest //= n
        index = tuple(reversed(index))
        target = total if out is None else out
        value = total[index].astype(jnp.float32) + more[index].astype(jnp.float32)
        target[index] = value.astype(target.dtype)


def add_many(total, more):
    lead = total.shape[:-2]

    def one(flat, _):
        index = []
        rest = flat
        for n in reversed(lead):
            index.append(rest % n)
            rest = rest // n
        index = tuple(reversed(index))
        total[index] = (total[index].astype(jnp.float32) + more[index].astype(jnp.float32)).astype(
            total.dtype
        )
        return 0

    lax.fori_loop(0, math.prod(lead), one, 0)


def scatter_steps(place, links, part, total, core_in, slots, out, order, local_sem):
    sizes, at = place.sizes, place.at
    half = part.shape[-1] // 2
    local = pltpu.make_async_copy(part.at[:, at["c"]], total, local_sem)
    local.start()
    copy = links.copy(part.at[:, 1 - at["c"]], core_in, place.device("c", 1 - at["c"]))
    yield
    local.wait()
    copy.wait()
    add_many(total, core_in)
    known = {}

    def view(values, columns=None):
        index = []
        for dim in "yab":
            index.append(
                pl.ds(values[dim], 1) if dim in values else pl.ds(0, sizes[dim])
            )
        if columns is not None:
            index += [slice(None), pl.ds(columns[0], columns[1])]
        return total.at[tuple(index)]

    slots = list(slots)
    for dim in order:
        n = sizes[dim]
        here = dict(known)
        here[dim] = at[dim]
        if n == 2:
            there = dict(known)
            there[dim] = 1 - at[dim]
            slot = slots.pop(0)
            copy = links.copy(view(there), slot, place.device(dim, 1 - at[dim]))
            yield
            copy.wait()
            add_many(view(here), slot)
        elif n == 4:
            right, left = place.shift(dim, 1), place.shift(dim, -1)
            to_right, to_left = place.device(dim, right), place.device(dim, left)
            near_right, near_left, far = dict(known), dict(known), dict(known)
            near_right[dim], near_left[dim], far[dim] = right, left, place.shift(dim, 2)
            half_a, half_b, whole_a, whole_b = slots[:4]
            slots = slots[4:]
            first = links.copy(view(far, (0, half)), half_a, to_right)
            second = links.copy(view(far, (half, half)), half_b, to_left)
            yield
            first.wait()
            second.wait()
            add_many(view(near_right, (0, half)), half_a)
            add_many(view(near_left, (half, half)), half_b)
            third = links.copy(view(near_right), whole_a, to_right)
            fourth = links.copy(view(near_left), whole_b, to_left)
            yield
            third.wait()
            fourth.wait()
            add_many(view(here), whole_a)
            add_many(view(here), whole_b)
        known = here
    yield
    out[...] = total[at["y"], at["a"], at["b"]].astype(out.dtype)


def slot_shapes(sizes, order, rows, columns):
    lead = {d: sizes[d] for d in "yab"}
    shapes = []
    for dim in order:
        n = lead[dim]
        lead[dim] = 1
        whole = (lead["y"], lead["a"], lead["b"], rows, columns)
        split = whole[:-1] + (columns // 2,)
        if n == 2:
            shapes.append(whole)
        elif n == 4:
            shapes += [split, split, whole, whole]
    return shapes


SCATTER_COPIES = 7


def scatter_kernel(sizes, orders, slot_counts, *refs):
    count = len(orders)
    parts, outs = refs[:count], refs[count : 2 * count]
    rest = list(refs[2 * count :])
    totals, core_ins = rest[:count], rest[count : 2 * count]
    rest = rest[2 * count :]
    slots = []
    for n in slot_counts:
        slots.append(rest[:n])
        rest = rest[n:]
    send_sem, recv_sem, local_sem = rest
    place = Place(sizes)
    place.greet()
    links = Links(send_sem, recv_sem)
    run_all(
        scatter_steps(
            place, links, parts[i], totals[i], core_ins[i], slots[i], outs[i], orders[i], local_sem.at[i]
        )
        for i in range(count)
    )


def scatter_all(sizes, parts, orders, collective_id):
    count = len(parts)
    lead = (sizes["y"], 2, sizes["a"], sizes["b"])
    devices = math.prod(lead)
    parts = [p.reshape(lead + (p.shape[0] // devices, p.shape[1])) for p in parts]
    blocks = [p.shape[4:] for p in parts]
    core_lead = (lead[0],) + lead[2:]
    slots = [slot_shapes(sizes, o, *b) for o, b in zip(orders, blocks)]
    total = SCATTER_COPIES * count
    planes = [pltpu.VMEM(core_lead + b, jnp.bfloat16) for b in blocks]
    return pl.pallas_call(
        partial(scatter_kernel, sizes, orders, [len(s) for s in slots]),
        out_shape=[jax.ShapeDtypeStruct(b, jnp.float32) for b in blocks],
        in_specs=[pl.BlockSpec(memory_space=pl.ANY)] * count,
        out_specs=[pl.BlockSpec(memory_space=pltpu.VMEM)] * count,
        scratch_shapes=planes
        + planes
        + [pltpu.VMEM(s, jnp.bfloat16) for group in slots for s in group]
        + [
            pltpu.SemaphoreType.DMA((total,)),
            pltpu.SemaphoreType.DMA((total,)),
            pltpu.SemaphoreType.DMA((count,)),
        ],
        compiler_params=pltpu.CompilerParams(
            collective_id=collective_id, has_side_effects=True, vmem_limit_bytes=VMEM_LIMIT
        ),
        cost_estimate=pl.CostEstimate(
            flops=0, bytes_accessed=sum(p.size for p in parts) * 2, transcendentals=0
        ),
    )(*parts)


def make_kernel(log_step, state_out, log_rate, blocks, length):
    step_size = jnp.exp(log_step)[:, None]
    decay_rate = step_size * jnp.exp(log_rate)
    weight = state_out * step_size

    def one_block(block_first):
        places = block_first + jnp.arange(length).astype(log_step.dtype)
        decays = jnp.exp(-decay_rate[None, :, :] * places[:, None, None])
        return jnp.sum(decays * weight[None, :, :], axis=2)

    block_starts = (jnp.arange(blocks) * length).astype(log_step.dtype)
    return lax.map(jax.checkpoint(one_block), block_starts).reshape(blocks * length, -1)


def dft_tables(block_len):
    period = 2 * block_len
    freqs = jnp.arange(block_len + 1)
    times = jnp.arange(period)
    turns = freqs[:, None] * times[None, :] % period
    angles = turns.astype(jnp.float32) * (2.0 * math.pi / period)
    cosine_table = jnp.cos(angles)
    sine_table = jnp.sin(angles)
    edge = (freqs == 0) | (freqs == block_len)
    weights = (jnp.where(edge, 1.0, 2.0) / period).astype(jnp.float32)[:, None]
    return (cosine_table, sine_table, cosine_table * weights, sine_table * weights)


def to_spectrum(signal, cosine_table, sine_table):
    real_part = jnp.einsum("ft,ntc->nfc", cosine_table, signal, precision=lax.Precision.HIGH)
    imag_part = -jnp.einsum("ft,ntc->nfc", sine_table, signal, precision=lax.Precision.HIGH)
    return (real_part, imag_part)


def to_time(real_part, imag_part, inverse_cosine, inverse_sine):
    cos_terms = jnp.einsum("ft,nfc->ntc", inverse_cosine, real_part, precision=lax.Precision.HIGH)
    sin_terms = jnp.einsum("ft,nfc->ntc", inverse_sine, imag_part, precision=lax.Precision.HIGH)
    return cos_terms - sin_terms


def kernel_segments(kernel, block_count):
    block_len = kernel.shape[0] // block_count
    feature_width = kernel.shape[1]
    padded = jnp.concatenate([jnp.zeros((block_len, feature_width), jnp.float32), kernel], axis=0)
    upper = padded[block_len:].reshape(block_count, block_len, feature_width)
    lower = padded[: block_count * block_len].reshape(block_count, block_len, feature_width)
    return jnp.concatenate([upper, lower], axis=1)


def segments_to_kernel(segment_grad):
    block_count = segment_grad.shape[0]
    block_len = segment_grad.shape[1] // 2
    feature_width = segment_grad.shape[2]
    upper_grad = segment_grad[:, :block_len].reshape(block_count * block_len, feature_width)
    lower_grad = segment_grad[1:, block_len:].reshape((block_count - 1) * block_len, feature_width)
    return upper_grad + jnp.concatenate(
        [lower_grad, jnp.zeros((block_len, feature_width), jnp.float32)], axis=0
    )


def mix_forward(kernel_spec, signal_spec, starts):
    kernel_real, kernel_imag = kernel_spec
    signal_real, signal_imag = signal_spec
    block_count = starts.shape[0]
    places = jnp.arange(block_count)

    def add_offset(offset, totals):
        total_real, total_imag = totals
        moved_real = jnp.roll(signal_real, offset, axis=0)
        moved_imag = jnp.roll(signal_imag, offset, axis=0)
        taps_real = lax.dynamic_index_in_dim(kernel_real, offset, 0, keepdims=False)
        taps_imag = lax.dynamic_index_in_dim(kernel_imag, offset, 0, keepdims=False)
        usable = (places - offset >= starts)[:, None, None]
        part_real = taps_real * moved_real - taps_imag * moved_imag
        part_imag = taps_real * moved_imag + taps_imag * moved_real
        return (
            total_real + jnp.where(usable, part_real, 0.0),
            total_imag + jnp.where(usable, part_imag, 0.0),
        )

    empty = jnp.zeros_like(signal_real)
    return lax.fori_loop(0, kernel_real.shape[0], add_offset, (empty, empty))


def mix_backward(kernel_spec, grad_spec, starts):
    kernel_real, kernel_imag = kernel_spec
    grad_real, grad_imag = grad_spec
    block_count = starts.shape[0]
    places = jnp.arange(block_count)

    def add_offset(offset, totals):
        total_real, total_imag = totals
        moved_real = jnp.roll(grad_real, -offset, axis=0)
        moved_imag = jnp.roll(grad_imag, -offset, axis=0)
        taps_real = lax.dynamic_index_in_dim(kernel_real, offset, 0, keepdims=False)
        taps_imag = lax.dynamic_index_in_dim(kernel_imag, offset, 0, keepdims=False)
        usable = jnp.roll(places - offset >= starts, -offset)[:, None, None]
        part_real = taps_real * moved_real + taps_imag * moved_imag
        part_imag = taps_real * moved_imag - taps_imag * moved_real
        return (
            total_real + jnp.where(usable, part_real, 0.0),
            total_imag + jnp.where(usable, part_imag, 0.0),
        )

    empty = jnp.zeros_like(grad_real)
    return lax.fori_loop(0, kernel_real.shape[0], add_offset, (empty, empty))


def mix_kernel(signal_spec, grad_spec, starts, offset_count):
    signal_real, signal_imag = signal_spec
    grad_real, grad_imag = grad_spec
    block_count = starts.shape[0]
    places = jnp.arange(block_count)

    def add_offset(offset, totals):
        total_real, total_imag = totals
        moved_real = jnp.roll(signal_real, offset, axis=0)
        moved_imag = jnp.roll(signal_imag, offset, axis=0)
        usable = (places - offset >= starts)[:, None, None]
        part_real = jnp.sum(
            jnp.where(usable, grad_real * moved_real + grad_imag * moved_imag, 0.0), axis=0
        )
        part_imag = jnp.sum(
            jnp.where(usable, grad_imag * moved_real - grad_real * moved_imag, 0.0), axis=0
        )
        return (
            lax.dynamic_update_index_in_dim(total_real, part_real, offset, 0),
            lax.dynamic_update_index_in_dim(total_imag, part_imag, offset, 0),
        )

    empty = jnp.zeros((offset_count,) + signal_real.shape[1:], jnp.float32)
    return lax.fori_loop(0, offset_count, add_offset, (empty, empty))


def conv_forward(values, kernel_spec, starts, tables):
    (
        fwd_cos_half,
        fwd_sin_half,
        inv_cos_half,
        inv_sin_half,
        fwd_cos_full,
        fwd_sin_full,
        inv_cos_full,
        inv_sin_full,
    ) = tables
    block_count = starts.shape[0]
    blocks = values.reshape(block_count, -1, values.shape[1])
    signal_spec = to_spectrum(blocks, fwd_cos_half, fwd_sin_half)
    mixed_real, mixed_imag = mix_forward(kernel_spec, signal_spec, starts)
    return (
        to_time(mixed_real, mixed_imag, inv_cos_half, inv_sin_half).reshape(values.shape),
        signal_spec,
    )


def conv_backward(grad_values, kernel_spec, signal_spec, starts, tables):
    (
        fwd_cos_half,
        fwd_sin_half,
        inv_cos_half,
        inv_sin_half,
        fwd_cos_full,
        fwd_sin_full,
        inv_cos_full,
        inv_sin_full,
    ) = tables
    block_count = starts.shape[0]
    blocks = grad_values.reshape(block_count, -1, grad_values.shape[1])
    grad_spec = to_spectrum(blocks, fwd_cos_half, fwd_sin_half)
    back_real, back_imag = mix_backward(kernel_spec, grad_spec, starts)
    signal_grad = to_time(back_real, back_imag, inv_cos_half, inv_sin_half).reshape(
        grad_values.shape
    )
    seg_real, seg_imag = mix_kernel(signal_spec, grad_spec, starts, kernel_spec[0].shape[0])
    segment_grad = to_time(seg_real, seg_imag, inv_cos_full, inv_sin_full)
    return (signal_grad, segments_to_kernel(segment_grad))


def norm_parts(values, norm_gain, norm_bias):
    row_mean = jnp.mean(values, axis=-1, keepdims=True)
    centred = values - row_mean
    row_var = jnp.mean(centred * centred, axis=-1, keepdims=True)
    inverse = lax.rsqrt(row_var + 1e-05)
    unit_rows = centred * inverse
    return (
        unit_rows * norm_gain.astype(jnp.float32) + norm_bias.astype(jnp.float32),
        unit_rows,
        inverse,
    )


def norm_back(grad_out, unit_rows, inverse, norm_gain):
    scaled = grad_out * norm_gain.astype(jnp.float32)
    mean_plain = jnp.mean(scaled, axis=-1, keepdims=True)
    mean_unit = jnp.mean(scaled * unit_rows, axis=-1, keepdims=True)
    input_grad = inverse * (scaled - mean_plain - unit_rows * mean_unit)
    return (input_grad, jnp.sum(grad_out * unit_rows, axis=0), jnp.sum(grad_out, axis=0))


def matmul_rows(left, right):
    return jnp.dot(left, right, preferred_element_type=jnp.float32)


def matmul_back(left, right):
    return jnp.einsum("td,cd->tc", left, right, preferred_element_type=jnp.float32)


def matmul_weight(left, right):
    return jnp.einsum("tc,td->cd", left, right, preferred_element_type=jnp.float32)


def shards(
    tokens,
    doc_start,
    attn_gain,
    attn_bias,
    w_query,
    w_key,
    w_value,
    shift_taps,
    log_step,
    state_out,
    log_rate,
    w_output,
    mlp_gain,
    mlp_bias,
    w_up,
    w_down,
    cotangent,
):
    sizes = mesh_dims(lax.axis_size("dp"), lax.axis_size("fsdp"))
    fits = kernels_fit(sizes, w_query.shape[0])
    block_count = doc_start.shape[0]
    block_len = tokens.shape[0] // block_count
    kernel_fn = partial(make_kernel, blocks=block_count, length=block_len)
    own_kernel, kernel_pull = jax.vjp(
        kernel_fn,
        log_step.astype(jnp.float32),
        state_out.astype(jnp.float32),
        log_rate.astype(jnp.float32),
    )
    own_rows = attn_gain.shape[0]
    tap_count = shift_taps.shape[1]
    small = jnp.concatenate(
        [shift_taps]
        + [v[:, None] for v in (attn_gain, attn_bias, mlp_gain, mlp_bias)]
        + [jnp.zeros((own_rows, 256 - 4 - tap_count), jnp.bfloat16)],
        axis=1,
    )
    owned = (w_query, w_key, w_value, small, own_kernel.T.astype(jnp.bfloat16), w_output, w_up, w_down)
    if fits:
        gathered = gather_all(sizes, owned, ORDERS, 0)
    else:
        gathered = [lax.all_gather(v, ("dp", "fsdp"), axis=0, tiled=True) for v in owned]
    (
        query_weight,
        key_weight,
        value_weight,
        small_all,
        kernel_all,
        output_weight,
        up_weight,
        down_weight,
    ) = gathered
    taps_weight = small_all[:, :tap_count]
    gain_first, bias_first, gain_second, bias_second = (small_all[:, tap_count + i] for i in range(4))
    kernel_long = kernel_all.astype(jnp.float32).T
    fwd_cos, fwd_sin, inv_cos, inv_sin = dft_tables(block_len)
    tables = (
        fwd_cos[:, :block_len],
        fwd_sin[:, :block_len],
        inv_cos[:, :block_len],
        inv_sin[:, :block_len],
        fwd_cos,
        fwd_sin,
        inv_cos,
        inv_sin,
    )
    kernel_shift = jnp.pad(
        taps_weight.astype(jnp.float32).T, ((0, 2 * block_len - tap_count), (0, 0))
    )
    long_spec = to_spectrum(kernel_segments(kernel_long, block_count), fwd_cos, fwd_sin)
    shift_spec = to_spectrum(kernel_segments(kernel_shift, 2), fwd_cos, fwd_sin)
    inputs = tokens.astype(jnp.float32)
    normed_first, unit_first, inverse_first = norm_parts(inputs, gain_first, bias_first)
    normed_first_low = normed_first.astype(jnp.bfloat16)
    query = matmul_rows(normed_first_low, query_weight)
    keyed = matmul_rows(normed_first_low, key_weight)
    valued = matmul_rows(normed_first_low, value_weight)
    shifted, keyed_spec = conv_forward(keyed, shift_spec, doc_start, tables)
    product = shifted * valued
    mixed, product_spec = conv_forward(product, long_spec, doc_start, tables)
    gated_low = (query * mixed).astype(jnp.bfloat16)
    middle = inputs + matmul_rows(gated_low, output_weight)
    normed_second, unit_second, inverse_second = norm_parts(middle, gain_second, bias_second)
    normed_second_low = normed_second.astype(jnp.bfloat16)
    hidden = matmul_rows(normed_second_low, up_weight)
    active_low = jax.nn.gelu(hidden, approximate=False).astype(jnp.bfloat16)
    layer_out = (middle + matmul_rows(active_low, down_weight)).astype(jnp.bfloat16)
    down_grad = matmul_weight(active_low, cotangent)
    grad_active = matmul_back(cotangent, down_weight)
    cumulative = 0.5 * (1.0 + lax.erf(hidden * (1.0 / math.sqrt(2.0))))
    density = jnp.exp(-0.5 * hidden * hidden) * (1.0 / math.sqrt(2.0 * math.pi))
    grad_hidden_low = (grad_active * (cumulative + hidden * density)).astype(jnp.bfloat16)
    up_grad = matmul_weight(normed_second_low, grad_hidden_low)
    grad_normed_second = matmul_back(grad_hidden_low, up_weight)
    grad_middle_norm, mlp_gain_grad, mlp_bias_grad = norm_back(
        grad_normed_second, unit_second, inverse_second, gain_second
    )
    grad_middle = cotangent.astype(jnp.float32) + grad_middle_norm
    grad_branch_low = grad_middle.astype(jnp.bfloat16)
    output_grad = matmul_weight(gated_low, grad_branch_low)
    grad_gated = matmul_back(grad_branch_low, output_weight)
    grad_query_low = (grad_gated * mixed).astype(jnp.bfloat16)
    grad_mixed = grad_gated * query
    grad_product, grad_kernel_long = conv_backward(
        grad_mixed, long_spec, product_spec, doc_start, tables
    )
    grad_shifted = grad_product * valued
    grad_value_low = (grad_product * shifted).astype(jnp.bfloat16)
    grad_keyed, grad_kernel_shift = conv_backward(
        grad_shifted, shift_spec, keyed_spec, doc_start, tables
    )
    grad_keyed_low = grad_keyed.astype(jnp.bfloat16)
    taps_grad = grad_kernel_shift[:tap_count].T
    query_grad = matmul_weight(normed_first_low, grad_query_low)
    key_grad = matmul_weight(normed_first_low, grad_keyed_low)
    value_grad = matmul_weight(normed_first_low, grad_value_low)
    grad_normed_first = (
        matmul_back(grad_query_low, query_weight)
        + matmul_back(grad_keyed_low, key_weight)
        + matmul_back(grad_value_low, value_weight)
    )
    grad_inputs_norm, attn_gain_grad, attn_bias_grad = norm_back(
        grad_normed_first, unit_first, inverse_first, gain_first
    )
    tokens_grad = grad_middle + grad_inputs_norm
    small_grad = jnp.concatenate(
        [taps_grad]
        + [v[:, None] for v in (attn_gain_grad, attn_bias_grad, mlp_gain_grad, mlp_bias_grad)]
        + [jnp.zeros((taps_grad.shape[0], 256 - 4 - tap_count), jnp.float32)],
        axis=1,
    )
    parts = (query_grad, key_grad, value_grad, small_grad, grad_kernel_long.T, output_grad, up_grad, down_grad)
    parts = [p.astype(jnp.bfloat16) for p in parts]
    if fits:
        sums = scatter_all(sizes, parts, ORDERS, 1)
    else:
        sums = [
            lax.psum_scatter(p, ("dp", "fsdp"), scatter_dimension=0, tiled=True).astype(jnp.float32)
            for p in parts
        ]
    query_part, key_part, value_part, small_part, kernel_part, output_part, up_part, down_part = sums
    step_part, state_part, rate_part = kernel_pull(kernel_part.T)
    return (
        layer_out,
        tokens_grad,
        small_part[:, tap_count],
        small_part[:, tap_count + 1],
        query_part,
        key_part,
        value_part,
        small_part[:, :tap_count],
        step_part,
        state_part,
        rate_part,
        output_part,
        small_part[:, tap_count + 2],
        small_part[:, tap_count + 3],
        up_part,
        down_part,
    )


def solution(mesh):
    placed = (
        P(("dp", "fsdp"), None),
        P(("dp", "fsdp")),
        P(("dp", "fsdp")),
        P(("dp", "fsdp")),
        P(("dp", "fsdp"), None),
        P(("dp", "fsdp"), None),
        P(("dp", "fsdp"), None),
        P(("dp", "fsdp"), None),
        P(("dp", "fsdp")),
        P(("dp", "fsdp"), None),
        P(("dp", "fsdp"), None),
        P(("dp", "fsdp"), None),
        P(("dp", "fsdp")),
        P(("dp", "fsdp")),
        P(("dp", "fsdp"), None),
        P(("dp", "fsdp"), None),
        P(("dp", "fsdp"), None),
    )
    return jax.shard_map(
        shards,
        mesh=mesh,
        in_specs=placed,
        out_specs=(
            P(("dp", "fsdp"), None),
            P(("dp", "fsdp"), None),
            P(("dp", "fsdp")),
            P(("dp", "fsdp")),
            P(("dp", "fsdp"), None),
            P(("dp", "fsdp"), None),
            P(("dp", "fsdp"), None),
            P(("dp", "fsdp"), None),
            P(("dp", "fsdp")),
            P(("dp", "fsdp"), None),
            P(("dp", "fsdp"), None),
            P(("dp", "fsdp"), None),
            P(("dp", "fsdp")),
            P(("dp", "fsdp")),
            P(("dp", "fsdp"), None),
            P(("dp", "fsdp"), None),
        ),
        check_vma=False,
    )
```
